256 devices in a mesh: seq: 128 (over y, z_lo, x, core), ch: 2 (over z_hi).
Axes of the slice: x: 4, y: 4, z: 8 (z_hi: 2, z_lo: 4; z = z_hi * 4 + z_lo), core: 2. Of those that a mesh axis runs over, the one named last changes fastest.
Arguments:
- signal: bfloat16 [524288, 1024], P('seq', 'ch'), may hold values from -6 to 6
- twiddle: float32 [512, 1024], P('seq'), may hold values from -4 to 4
- row_factor: bfloat16 [1024, 1024], replicated, may hold values from -0.1875 to 0.1875
- col_factor: bfloat16 [512, 512], replicated, may hold values from -0.25 to 0.25
- block_mix: bfloat16 [64, 16, 16], P('ch'), may hold values from -1.5 to 1.5
- spread_mix: bfloat16 [16, 64, 64], replicated, may hold values from -0.75 to 0.75
- gate_scale: float32 [1024], P('ch'), may hold values from 0.5 to 2
Outputs:
- output: bfloat16 [524288, 1024], P('seq', 'ch')
The draws below stay inside these ranges and needn't reach their ends.
All inputs are finite; a program needn't handle non-finite values.
Results may differ from the reference program's by a relative error of at most 0.0056.
Values may be sent and summed in bfloat16 or wider, within the bound.
A program may use at most 128 MiB of HBM per device.

```python
import math
import jax
import jax.numpy as jnp
from jax import lax

LA = 512
LB = 1024
D = 1024
BLOCK = 16
GROUPS = 64
SEQ_LEN = 524288


def block_levels(rng, shape, split, least, largest):
    def one(dim, parts):
        heights = jax.random.uniform(jax.random.fold_in(jax.random.fold_in(rng, 6), dim), (parts,), jnp.float32, least / len(split), largest / len(split))
        return jnp.repeat(jnp.exp(heights), shape[dim] // parts).reshape((-1,) + (1,) * (len(shape) - dim - 1))

    loudness = one(*split[0])
    for cut in split[1:]:
        loudness = loudness * one(*cut)
    return loudness


def noise(rng, dims, scale, most, pieces=(), kind=jnp.bfloat16):
    values = scale * jax.random.normal(rng, dims, jnp.float32)
    if pieces:
        values = values * block_levels(rng, dims, pieces, -0.22, 0.18)
    return jnp.clip(values, -most, most).astype(kind)


def setup_inputs(seed: int = 0) -> dict:
    seeds = jax.random.split(jax.random.key(seed), 8)
    signal = noise(seeds[0], (SEQ_LEN, D), 1.0, 6.0, ((0, 128), (1, 2)))
    twiddle = noise(seeds[1], (LA, LB), 1.0, 4.0, ((0, 128),), jnp.float32)
    row_factor = noise(seeds[2], (LB, LB), LB ** -0.5, 0.1875)
    col_factor = noise(seeds[3], (LA, LA), LA ** -0.5, 0.25)
    block_mix = noise(seeds[4], (GROUPS, BLOCK, BLOCK), BLOCK ** -0.5, 1.5, ((0, 2),))
    spread_mix = noise(seeds[5], (BLOCK, GROUPS, GROUPS), GROUPS ** -0.5, 0.75)
    gate_scale = jnp.clip(jnp.exp(math.log(2.0) - 1.3862944 * jax.random.uniform(seeds[6], (D,), jnp.float32) ** block_levels(seeds[6], (D,), ((0, 2),), -0.2, 0.2)), 0.5, 2.0)
    return {"signal": signal, "twiddle": twiddle, "row_factor": row_factor, "col_factor": col_factor, "block_mix": block_mix, "spread_mix": spread_mix, "gate_scale": gate_scale}


chan_span = 64
token_span = 4096


def reference(signal, twiddle, row_factor, col_factor, block_mix, spread_mix, gate_scale):
    lattice = signal.reshape(LA, LB, D // chan_span, chan_span).transpose(2, 0, 1, 3)
    row_weights = row_factor.astype(jnp.float32)
    col_weights = col_factor.astype(jnp.float32)

    def seq_mix(channel_block):
        mixed_rows = jnp.einsum("ijc,jk->ikc", channel_block.astype(jnp.float32), row_weights)
        mixed_rows = (mixed_rows * twiddle[:, :, None]).astype(jnp.bfloat16)
        return jnp.einsum("im,ikc->mkc", col_weights, mixed_rows.astype(jnp.float32)).astype(jnp.bfloat16)

    mixed = lax.map(seq_mix, lattice)
    mixed = mixed.transpose(1, 2, 0, 3).reshape(SEQ_LEN, D)
    block_weights = block_mix.astype(jnp.float32)
    spread_weights = spread_mix.astype(jnp.float32)

    def chan_mix(operands):
        mixed_part, signal_part = operands
        blocks_view = mixed_part.astype(jnp.float32).reshape(-1, GROUPS, BLOCK)
        blocked = jnp.einsum("tpq,pqr->tpr", blocks_view, block_weights).astype(jnp.bfloat16)
        spread = jnp.einsum("tpr,rps->tsr", blocked.astype(jnp.float32), spread_weights).astype(jnp.bfloat16)
        spread = spread.reshape(-1, D).astype(jnp.float32)
        signal32 = signal_part.astype(jnp.float32)
        return (signal32 + jax.nn.silu(gate_scale[None, :] * signal32) * spread).astype(jnp.bfloat16)

    count = SEQ_LEN // token_span
    result = lax.map(chan_mix, (mixed.reshape(count, token_span, D), signal.reshape(count, token_span, D)))
    return result.reshape(SEQ_LEN, D)
```

```python
import jax
import jax.numpy as jnp
from jax import lax
from jax.sharding import PartitionSpec as P

F32 = jnp.float32
BF16 = jnp.bfloat16


def channel_matrix(block_mix, spread_mix):
    groups, width, _ = block_mix.shape
    chans = groups * width
    col = lax.broadcasted_iota(jnp.int32, (width, chans), 1) % width
    tile = (col == lax.broadcasted_iota(jnp.int32, (width, chans), 0)).astype(BF16)
    row = lax.broadcasted_iota(jnp.int32, (chans, groups), 0) // width
    repeat = (row == lax.broadcasted_iota(jnp.int32, (chans, groups), 1)).astype(BF16)
    spread_rows = spread_mix.transpose(1, 2, 0).reshape(groups, chans)
    blocks = jnp.dot(block_mix.reshape(chans, width), tile, preferred_element_type=F32)
    spreads = jnp.dot(repeat, spread_rows, preferred_element_type=F32)
    return (blocks * spreads).astype(BF16)


def per_device(signal, twiddle, row_factor, col_factor, block_mix, spread_mix, gate_scale):
    seq_count = lax.axis_size("seq")
    ch_count = lax.axis_size("ch")
    count = seq_count * ch_count
    rows, cols = twiddle.shape
    width = signal.shape[1]
    each = cols // count
    lattice = signal.reshape(rows, cols, width)
    block_all = lax.all_gather(block_mix, "ch", axis=0, tiled=True)
    chan = channel_matrix(block_all, spread_mix)
    mixed = jnp.einsum("ijc,jk->kic", lattice, row_factor, preferred_element_type=F32)
    mixed = (mixed * twiddle.T[:, :, None]).astype(BF16).reshape(count, each * rows, width)
    arrived = lax.all_to_all(mixed, ("seq", "ch"), split_axis=0, concat_axis=0, tiled=True)
    arrived = arrived.reshape(seq_count, ch_count, each, rows, width)
    weights = col_factor.reshape(seq_count, rows, seq_count * rows)
    mixed_cols = jnp.einsum("slm,sgklc->mkgc", weights, arrived, preferred_element_type=F32).astype(BF16)
    spread = jnp.dot(mixed_cols.reshape(-1, ch_count * width), chan, preferred_element_type=F32).astype(BF16)
    spread = spread.reshape(seq_count, rows * each, ch_count, width).transpose(0, 2, 1, 3)
    spread = spread.reshape(count, rows * each, width)
    back = lax.all_to_all(spread, ("seq", "ch"), split_axis=0, concat_axis=0, tiled=True)
    back = back.reshape(count, rows, each, width).transpose(1, 0, 2, 3).reshape(signal.shape)
    signal32 = signal.astype(F32)
    gated = jax.nn.silu(gate_scale[None, :] * signal32) * back.astype(F32)
    return (signal32 + gated).astype(BF16)


def solution(mesh):
    placed = (P("seq", "ch"), P("seq", None), P(), P(), P("ch", None, None), P(), P("ch"))
    return jax.shard_map(
        per_device, mesh=mesh, in_specs=placed, out_specs=P("seq", "ch"), check_vma=False
    )
```

```python
import jax
import jax.numpy as jnp
from jax import lax
from jax.experimental import pallas as pl
from jax.experimental.pallas import tpu as pltpu
from jax.sharding import PartitionSpec as P

F32 = jnp.float32
BF16 = jnp.bfloat16


def channel_matrix(block_mix, spread_mix):
    groups, width, _ = block_mix.shape
    chans = groups * width
    col = lax.broadcasted_iota(jnp.int32, (width, chans), 1) % width
    tile = (col == lax.broadcasted_iota(jnp.int32, (width, chans), 0)).astype(BF16)
    row = lax.broadcasted_iota(jnp.int32, (chans, groups), 0) // width
    repeat = (row == lax.broadcasted_iota(jnp.int32, (chans, groups), 1)).astype(BF16)
    spread_rows = spread_mix.transpose(1, 2, 0).reshape(groups, chans)
    blocks = jnp.dot(block_mix.reshape(chans, width), tile, preferred_element_type=F32)
    spreads = jnp.dot(repeat, spread_rows, preferred_element_type=F32)
    return (blocks * spreads).astype(BF16)


def exchange_kernel(send, recv, own_sem, send_sem, recv_sem):
    seq, ch = lax.axis_index("seq"), lax.axis_index("ch")
    mine = seq * 2 + ch
    own = pltpu.make_async_copy(send.at[mine], recv.at[mine], own_sem)
    own.start()

    def body(n, carry):
        other = (mine + n + 1) % 256
        pltpu.make_async_remote_copy(
            src_ref=send.at[other],
            dst_ref=recv.at[mine],
            send_sem=send_sem,
            recv_sem=recv_sem,
            device_id=(other // 2, other % 2),
            device_id_type=pl.DeviceIdType.MESH,
        ).start()
        return carry

    lax.fori_loop(0, 255, body, 0)
    own.wait()
    pltpu.make_async_copy(send.at[0:255], send.at[0:255], send_sem).wait()
    pltpu.make_async_copy(recv.at[0:255], recv.at[0:255], recv_sem).wait()


def exchange(blocks):
    return pl.pallas_call(
        exchange_kernel,
        out_shape=jax.ShapeDtypeStruct(blocks.shape, blocks.dtype),
        in_specs=[pl.BlockSpec(memory_space=pl.ANY)],
        out_specs=pl.BlockSpec(memory_space=pl.ANY),
        scratch_shapes=[pltpu.SemaphoreType.DMA, pltpu.SemaphoreType.DMA, pltpu.SemaphoreType.DMA],
        compiler_params=pltpu.CompilerParams(has_side_effects=True),
    )(blocks)


def per_device(signal, twiddle, row_factor, col_factor, block_mix, spread_mix, gate_scale):
    seq_count = lax.axis_size("seq")
    ch_count = lax.axis_size("ch")
    count = seq_count * ch_count
    rows, cols = twiddle.shape
    width = signal.shape[1]
    each = cols // count
    lattice = signal.reshape(rows, cols, width)
    block_all = lax.all_gather(block_mix, "ch", axis=0, tiled=True)
    chan = channel_matrix(block_all, spread_mix)
    mixed = jnp.einsum("ijc,jk->kic", lattice, row_factor, preferred_element_type=F32)
    mixed = (mixed * twiddle.T[:, :, None]).astype(BF16).reshape(count, each * rows, width)
    arrived = exchange(mixed)
    arrived = arrived.reshape(seq_count, ch_count, each, rows, width)
    weights = col_factor.reshape(seq_count, rows, seq_count * rows)
    mixed_cols = jnp.einsum("slm,sgklc->mkgc", weights, arrived, preferred_element_type=F32).astype(BF16)
    spread = jnp.dot(mixed_cols.reshape(-1, ch_count * width), chan, preferred_element_type=F32).astype(BF16)
    spread = spread.reshape(seq_count, rows * each, ch_count, width).transpose(0, 2, 1, 3)
    spread = spread.reshape(count, rows * each, width)
    back = exchange(spread)
    back = back.reshape(count, rows, each, width).transpose(1, 0, 2, 3).reshape(signal.shape)
    signal32 = signal.astype(F32)
    gated = jax.nn.silu(gate_scale[None, :] * signal32) * back.astype(F32)
    return (signal32 + gated).astype(BF16)


def solution(mesh):
    placed = (P("seq", "ch"), P("seq", None), P(), P(), P("ch", None, None), P(), P("ch"))
    return jax.shard_map(
        per_device, mesh=mesh, in_specs=placed, out_specs=P("seq", "ch"), check_vma=False
    )
```

```python
import jax
import jax.numpy as jnp
from jax import lax
from jax.experimental import pallas as pl
from jax.experimental.pallas import tpu as pltpu
from jax.sharding import PartitionSpec as P

F32 = jnp.float32
BF16 = jnp.bfloat16
NT = (((1,), (1,)), ((), ()))
TN = (((0,), (0,)), ((), ()))


def iota(shape, dim):
    return lax.broadcasted_iota(jnp.int32, shape, dim)


def dot(a, b):
    return jnp.dot(a, b, preferred_element_type=F32)


def rows_at(ref, start, size):
    return ref.at[pl.ds(pl.multiple_of(start, 16), size)]


def pair_of(x, y):
    return (x % 2) * 4 + (y + 2 * (x // 2)) % 4


def z_offset(n):
    odd = n % 2
    step = odd * ((n + 1) // 2) + (1 - odd) * (8 - n // 2)
    return (step - 4 * jnp.where(n == 0, 1, 0) + jnp.where(n == 7, 4, 0)) % 8


def kernel(
    signal_hbm, rowf_hbm, colf_hbm, tw_ref, block_ref, mix_ref, gate_ref,
    out_hbm,
    signal, rowf, colf, send1, recv1, expand, chan, send2, recv2, out, gates,
    weave, unweave, blocks, spread_rows,
    load_sem, own_sem, send_sem, recv1_sem, recv2_sem, block_sem, out_sem,
):
    seq, ch = lax.axis_index("seq"), lax.axis_index("ch")
    y, x, core = seq // 32, (seq // 2) % 4, seq % 2
    z = ch * 4 + (seq // 8) % 4
    mine = pair_of(x, y) * 32 + (x // 2) * 16 + z * 2 + core

    loads = [pltpu.make_async_copy(rowf_hbm, rowf, load_sem.at[0])]
    for i in range(4):
        part = pl.ds(i * 1024, 1024)
        loads.append(pltpu.make_async_copy(signal_hbm.at[part], signal.at[part], load_sem.at[1 + i]))
    loads.append(pltpu.make_async_copy(colf_hbm, colf, load_sem.at[5]))
    for load in loads:
        load.start()

    o, s = iota((512, 512), 0), iota((512, 512), 1)
    weave[...] = (s == ((o >> 2) & 3) * 128 + (o >> 4) * 4 + (o & 3)).astype(F32).astype(BF16)
    unweave[...] = (o == ((s >> 2) & 3) * 128 + (s >> 4) * 4 + (s & 3)).astype(F32).astype(BF16)
    eye = iota((128, 128), 0) == iota((128, 128), 1)
    eye16 = eye.astype(F32).astype(BF16)

    eye_small = (iota((16, 16), 0) == iota((16, 16), 1)).astype(F32).astype(BF16)
    flipped = lax.dot_general(eye_small, block_ref[...], NT, preferred_element_type=F32)
    blocks[pl.ds(pl.multiple_of(ch * 16, 16), 16), :] = flipped.astype(BF16)
    block_copy = pltpu.make_async_remote_copy(
        src_ref=rows_at(blocks, ch * 16, 16), dst_ref=rows_at(blocks, ch * 16, 16),
        send_sem=block_sem.at[0], recv_sem=block_sem.at[1],
        device_id=(seq, 1 - ch), device_id_type=pl.DeviceIdType.MESH,
    )
    block_copy.start()
    for load in loads:
        load.wait()

    def send_tile(pair, source, target, recv_sem, source_row, own):
        def body(n, carry):
            half, far_core = n // 16, (n // 8) % 2
            far_z = (z + z_offset(n % 8)) % 8
            far_x, far_y = pair // 4 + 2 * half, (pair % 4 + 2 * half) % 4
            far_seq = far_y * 32 + (far_z % 4) * 8 + far_x * 2 + far_core
            far_ch = far_z // 4
            src = rows_at(source, source_row(half, far_z, far_core) * 16, 16)
            is_self = jnp.logical_and(far_seq == seq, far_ch == ch)

            @pl.when(is_self)
            def _():
                pltpu.make_async_copy(src, rows_at(target[0], target[1] * 16, 16), own).start()

            @pl.when(jnp.logical_not(is_self))
            def _():
                pltpu.make_async_remote_copy(
                    src_ref=src, dst_ref=rows_at(target[0], target[1] * 16, 16),
                    send_sem=send_sem, recv_sem=recv_sem,
                    device_id=(far_seq, far_ch), device_id_type=pl.DeviceIdType.MESH,
                ).start()

            return carry

        lax.fori_loop(0, 32, body, 0)

    def row_step(t, carry):
        pair = pair_of((x + t // 4) % 4, (y + t % 4) % 4)
        lanes = pl.ds(pl.multiple_of(pair * 128, 128), 128)
        weights = lax.dot_general(eye16, rowf[:, lanes], NT, preferred_element_type=F32).astype(BF16)
        parts = []
        for i in range(4):
            mixed = dot(weights, signal[i * 1024:(i + 1) * 1024, :])
            scale = jnp.sum(jnp.where(eye, tw_ref[i:i + 1, lanes], 0.0), axis=1, keepdims=True)
            parts.append((mixed * scale).astype(BF16))
        woven = dot(weave[...], jnp.concatenate(parts, axis=0)).astype(BF16)
        send1[pl.ds(pl.multiple_of(pair * 512, 512), 512), :] = woven
        send_tile(
            pair, send1, (recv1, ch * 128 + seq), recv1_sem,
            lambda half, far_z, far_core: pair * 32 + half * 16 + far_z * 2 + far_core, own_sem.at[0],
        )
        return carry

    lax.fori_loop(0, 8, row_step, 0)

    def gate_step(n, carry):
        part = pl.ds(pl.multiple_of(n * 64, 64), 64)
        v = gate_ref[...] * signal[part, :].astype(F32)
        gates[part, :] = v / (1.0 + jnp.exp(-v))
        return carry

    lax.fori_loop(0, 64, gate_step, 0)

    def expand_step(pair, carry):
        r = iota((256, 512), 0)
        half = r >> 7
        far_seq = ((pair % 4 + 2 * half) & 3) * 32 + ((r >> 5) & 3) * 8 + (pair // 4 + 2 * half) * 2 + ((r >> 4) & 1)
        pick = (iota((256, 512), 1) == far_seq * 4 + ((r >> 2) & 3)).astype(F32).astype(BF16)
        taken = lax.dot_general(pick, colf[...], NT, preferred_element_type=F32).astype(BF16)
        widen = (iota((128, 512), 0) == (iota((128, 512), 1) >> 2)).astype(F32).astype(BF16)
        same = (iota((256, 512), 0) & 3) == (iota((256, 512), 1) & 3)
        rows = pl.ds(pl.multiple_of(pair * 256, 256), 256)
        for j in range(4):
            wide = dot(taken[:, j * 128:(j + 1) * 128], widen)
            expand[rows, j * 512:(j + 1) * 512] = jnp.where(same, wide, 0.0).astype(BF16)
        return carry

    lax.fori_loop(0, 8, expand_step, 0)

    spread_rows[...] = jnp.zeros_like(spread_rows)

    def spread_step(r, carry):
        place = (iota((64, 1024), 1) == iota((64, 1024), 0) * 16 + r).astype(F32).astype(BF16)
        spread_rows[...] += dot(mix_ref[pl.ds(pl.multiple_of(r * 64, 64), 64), :], place)
        return carry

    lax.fori_loop(0, 16, spread_step, 0)
    block_copy.wait()
    tile = ((iota((16, 1024), 1) & 15) == iota((16, 1024), 0)).astype(F32).astype(BF16)
    repeat = ((iota((256, 16), 0) >> 4) == iota((256, 16), 1)).astype(F32).astype(BF16)
    for g in range(2):
        for q in range(2):
            left = lax.dot_general(
                blocks[g * 16:(g + 1) * 16, q * 256:(q + 1) * 256], tile, TN, preferred_element_type=F32
            )
            p0 = g * 32 + q * 16
            right = dot(repeat, spread_rows[p0:p0 + 16, :].astype(BF16))
            chan[p0 * 16:p0 * 16 + 256, :] = (left * right).astype(BF16)

    pltpu.make_async_copy(rows_at(recv1, 0, 16), rows_at(recv1, 0, 16), own_sem.at[0]).wait()
    pltpu.make_async_copy(rows_at(recv1, 0, 255 * 16), rows_at(recv1, 0, 255 * 16), recv1_sem).wait()

    def col_step(t, carry):
        pair = pair_of((x + t // 4) % 4, (y + t % 4) % 4)
        weights = expand[pl.ds(pl.multiple_of(pair * 256, 256), 256), :]
        low = dot(weights, recv1[0:2048, :]).astype(BF16)
        high = dot(weights, recv1[2048:4096, :]).astype(BF16)
        for h in range(2):
            cut = slice(h * 512, (h + 1) * 512)
            mixed = dot(low, chan[0:512, cut]) + dot(high, chan[512:1024, cut])
            send2[pl.ds(pl.multiple_of((pair * 2 + h) * 256, 256), 256), :] = mixed.astype(BF16)
        send_tile(
            pair, send2, (recv2, mine), recv2_sem.at[t],
            lambda half, far_z, far_core: (pair * 2 + far_z // 4) * 16 + half * 8 + (far_z % 4) * 2 + far_core,
            own_sem.at[1],
        )
        return carry

    lax.fori_loop(0, 8, col_step, 0)
    pltpu.make_async_copy(rows_at(recv2, 0, 16), rows_at(recv2, 0, 16), own_sem.at[1]).wait()

    def last_step(t, own):
        pair = pair_of((x - t // 4 + 4) % 4, (y - t % 4 + 4) % 4)
        got = rows_at(recv2, pair * 512, 512 - own)
        pltpu.make_async_copy(got, got, recv2_sem.at[t]).wait()
        spread = dot(unweave[...], recv2[pl.ds(pl.multiple_of(pair * 512, 512), 512), :])
        for i in range(4):
            part = pl.ds(pl.multiple_of(i * 1024 + pair * 128, 128), 128)
            out[part, :] = (signal[part, :].astype(F32) + gates[part, :] * spread[i * 128:(i + 1) * 128, :]).astype(BF16)
            pltpu.make_async_copy(out.at[part], out_hbm.at[part], out_sem).start()

    last_step(0, 16)

    def rest(t, carry):
        last_step(t, 0)
        return carry

    lax.fori_loop(1, 8, rest, 0)
    pltpu.make_async_copy(out, out_hbm, out_sem).wait()
    pltpu.make_async_copy(rows_at(send1, 0, 255 * 16), rows_at(send1, 0, 255 * 16), send_sem).wait()
    pltpu.make_async_copy(rows_at(send2, 0, 255 * 16), rows_at(send2, 0, 255 * 16), send_sem).wait()


def per_device(signal, twiddle, row_factor, col_factor, block_mix, spread_mix, gate_scale):
    groups, width, _ = block_mix.shape
    anywhere = pl.BlockSpec(memory_space=pl.ANY)
    inside = pl.BlockSpec(memory_space=pltpu.VMEM)
    dma = pltpu.SemaphoreType.DMA
    return pl.pallas_call(
        kernel,
        out_shape=jax.ShapeDtypeStruct(signal.shape, signal.dtype),
        in_specs=[anywhere, anywhere, anywhere, inside, inside, inside, inside],
        out_specs=anywhere,
        scratch_shapes=[
            pltpu.VMEM((4096, 512), BF16),
            pltpu.VMEM((1024, 1024), BF16),
            pltpu.VMEM((512, 512), BF16),
            pltpu.VMEM((4096, 512), BF16),
            pltpu.VMEM((4096, 512), BF16),
            pltpu.VMEM((2048, 2048), BF16),
            pltpu.VMEM((1024, 1024), BF16),
            pltpu.VMEM((4096, 512), BF16),
            pltpu.VMEM((4096, 512), BF16),
            pltpu.VMEM((4096, 512), BF16),
            pltpu.VMEM((4096, 512), F32),
            pltpu.VMEM((512, 512), BF16),
            pltpu.VMEM((512, 512), BF16),
            pltpu.VMEM((32, 512), BF16),
            pltpu.VMEM((64, 1024), F32),
            dma((6,)), dma((2,)), dma, dma, dma((8,)), dma((2,)), dma,
        ],
        compiler_params=pltpu.CompilerParams(has_side_effects=True, vmem_limit_bytes=58 << 20),
    )(
        signal, row_factor, col_factor, twiddle, block_mix.reshape(groups * width, width),
        spread_mix.reshape(-1, spread_mix.shape[2]), gate_scale.reshape(1, -1),
    )


def solution(mesh):
    placed = (P("seq", "ch"), P("seq", None), P(), P(), P("ch", None, None), P(), P("ch"))
    return jax.shard_map(
        per_device, mesh=mesh, in_specs=placed, out_specs=P("seq", "ch"), check_vma=False
    )
```

```python
import jax
import jax.numpy as jnp
from jax import lax
from jax.experimental import pallas as pl
from jax.experimental.pallas import tpu as pltpu
from jax.sharding import PartitionSpec as P

F32 = jnp.float32
BF16 = jnp.bfloat16
NT = (((1,), (1,)), ((), ()))
TN = (((0,), (0,)), ((), ()))


def iota(shape, dim):
    return lax.broadcasted_iota(jnp.int32, shape, dim)


def dot(a, b):
    return jnp.dot(a, b, preferred_element_type=F32)


def rows_at(ref, start, size):
    return ref.at[pl.ds(pl.multiple_of(start, 16), size)]


def pair_of(x, y):
    return (x % 2) * 4 + (y + 2 * (x // 2)) % 4


def z_offset(n):
    odd = n % 2
    step = odd * ((n + 1) // 2) + (1 - odd) * (8 - n // 2)
    return (step - 4 * jnp.where(n == 0, 1, 0) + jnp.where(n == 7, 4, 0)) % 8


def kernel(
    signal_hbm, rowf_hbm, colf_hbm, tw_ref, block_ref, mix_ref, gate_ref,
    out,
    signal, rowf, colf, send1, recv1, expand, chan, send2, recv2, gates,
    weave, unweave, blocks, spread_rows,
    load_sem, own_sem, send_sem, recv1_sem, recv2_sem, block_sem, plane_sem,
):
    seq, ch = lax.axis_index("seq"), lax.axis_index("ch")
    y, x, core = seq // 32, (seq // 2) % 4, seq % 2
    z = ch * 4 + (seq // 8) % 4
    mine = pair_of(x, y) * 32 + (x // 2) * 16 + z * 2 + core

    barrier = pltpu.get_barrier_semaphore()

    def greet(sem, dx, dy, dz, dc):
        far_z = (z + dz) % 8
        far_seq = (y + dy) % 4 * 32 + far_z % 4 * 8 + (x + dx) % 4 * 2 + (core + dc) % 2
        pl.semaphore_signal(
            sem, inc=1, device_id=(far_seq, far_z // 4), device_id_type=pl.DeviceIdType.MESH
        )

    def greet_plane(sem):
        def body(n, carry):
            greet(sem, (n + 1) % 4, (n + 1) // 4, 0, 0)
            return carry

        lax.fori_loop(0, 15, body, 0)

    def greet_line(n, carry):
        greet(barrier, 0, 0, (n + 1) // 2, (n + 1) % 2)
        return carry

    loads = []
    for i in range(4):
        part = pl.ds(i * 1024, 1024)
        loads.append(pltpu.make_async_copy(signal_hbm.at[part], signal.at[part], load_sem.at[1 + i]))
    loads = [pltpu.make_async_copy(rowf_hbm, rowf, load_sem.at[0])] + loads
    loads.append(pltpu.make_async_copy(colf_hbm, colf, load_sem.at[5]))
    lax.fori_loop(0, 15, greet_line, 0)
    greet_plane(barrier)
    for load in loads:
        load.start()

    o, s = iota((512, 512), 0), iota((512, 512), 1)
    weave[...] = (s == ((o >> 2) & 3) * 128 + (o >> 4) * 4 + (o & 3)).astype(F32).astype(BF16)
    eye = iota((128, 128), 0) == iota((128, 128), 1)
    eye16 = eye.astype(F32).astype(BF16)

    flipped = jnp.zeros((16, 512), F32)
    for q in range(16):
        place = (iota((32, 512), 1) == iota((32, 512), 0) * 16 + q).astype(F32).astype(BF16)
        flipped += dot(block_ref[q * 16:(q + 1) * 16, :], place)
    blocks[pl.ds(pl.multiple_of(ch * 16, 16), 16), :] = flipped.astype(BF16)
    block_copy = pltpu.make_async_remote_copy(
        src_ref=rows_at(blocks, ch * 16, 16), dst_ref=rows_at(blocks, ch * 16, 16),
        send_sem=block_sem.at[0], recv_sem=block_sem.at[1],
        device_id=(seq, 1 - ch), device_id_type=pl.DeviceIdType.MESH,
    )
    pl.semaphore_wait(barrier, 30)
    greet_plane(plane_sem)

    def send_tile(pair, source, target, recv_sem, source_row, own):
        def body(n, carry):
            half, far_core = n // 16, (n // 8) % 2
            far_z = (z + z_offset(n % 8)) % 8
            far_x, far_y = pair // 4 + 2 * half, (pair % 4 + 2 * half) % 4
            far_seq = far_y * 32 + (far_z % 4) * 8 + far_x * 2 + far_core
            far_ch = far_z // 4
            src = rows_at(source, source_row(half, far_z, far_core) * 16, 16)
            is_self = jnp.logical_and(far_seq == seq, far_ch == ch)

            @pl.when(is_self)
            def _():
                pltpu.make_async_copy(src, rows_at(target[0], target[1] * 16, 16), own).start()

            @pl.when(jnp.logical_not(is_self))
            def _():
                pltpu.make_async_remote_copy(
                    src_ref=src, dst_ref=rows_at(target[0], target[1] * 16, 16),
                    send_sem=send_sem, recv_sem=recv_sem,
                    device_id=(far_seq, far_ch), device_id_type=pl.DeviceIdType.MESH,
                ).start()

            return carry

        lax.fori_loop(0, 32, body, 0)

    def row_step(t, carry):
        pair = pair_of((x + t // 4) % 4, (y + t % 4) % 4)
        lanes = pl.ds(pl.multiple_of(pair * 128, 128), 128)

        @pl.when(t == 0)
        def _():
            loads[0].wait()

        weights = lax.dot_general(eye16, rowf[:, lanes], NT, preferred_element_type=F32).astype(BF16)
        parts = []
        for i in range(4):
            @pl.when(t == 0)
            def _():
                loads[1 + i].wait()

            mixed = dot(weights, signal[i * 1024:(i + 1) * 1024, :])
            scale = jnp.sum(jnp.where(eye, tw_ref[i:i + 1, lanes], 0.0), axis=1, keepdims=True)
            parts.append((mixed * scale).astype(BF16))
        woven = dot(weave[...], jnp.concatenate(parts, axis=0)).astype(BF16)
        send1[pl.ds(pl.multiple_of(pair * 512, 512), 512), :] = woven

        @pl.when(t == 0)
        def _():
            pl.semaphore_wait(plane_sem, 15)
            block_copy.start()

        send_tile(
            pair, send1, (recv1, ch * 128 + seq), recv1_sem,
            lambda half, far_z, far_core: pair * 32 + half * 16 + far_z * 2 + far_core, own_sem.at[0],
        )
        return carry

    lax.fori_loop(0, 8, row_step, 0)

    loads[5].wait()

    def gate_step(n, carry):
        part = pl.ds(pl.multiple_of(n * 64, 64), 64)
        v = gate_ref[...] * signal[part, :].astype(F32)
        gates[part, :] = v / (1.0 + jnp.exp(-v))
        return carry

    lax.fori_loop(0, 64, gate_step, 0)

    def expand_step(pair, carry):
        r = iota((256, 512), 0)
        half = r >> 7
        far_seq = ((pair % 4 + 2 * half) & 3) * 32 + ((r >> 5) & 3) * 8 + (pair // 4 + 2 * half) * 2 + ((r >> 4) & 1)
        pick = (iota((256, 512), 1) == far_seq * 4 + ((r >> 2) & 3)).astype(F32).astype(BF16)
        taken = lax.dot_general(pick, colf[...], NT, preferred_element_type=F32).astype(BF16)
        widen = (iota((128, 512), 0) == (iota((128, 512), 1) >> 2)).astype(F32).astype(BF16)
        same = (iota((256, 512), 0) & 3) == (iota((256, 512), 1) & 3)
        rows = pl.ds(pl.multiple_of(pair * 256, 256), 256)
        for j in range(4):
            wide = dot(taken[:, j * 128:(j + 1) * 128], widen)
            expand[rows, j * 512:(j + 1) * 512] = jnp.where(same, wide, 0.0).astype(BF16)
        return carry

    lax.fori_loop(0, 8, expand_step, 0)

    unweave[...] = (o == ((s >> 2) & 3) * 128 + (s >> 4) * 4 + (s & 3)).astype(F32).astype(BF16)
    spread_rows[...] = jnp.zeros_like(spread_rows)

    def spread_step(r, carry):
        place = (iota((64, 1024), 1) == iota((64, 1024), 0) * 16 + r).astype(F32).astype(BF16)
        spread_rows[...] += dot(mix_ref[pl.ds(pl.multiple_of(r * 64, 64), 64), :], place)
        return carry

    lax.fori_loop(0, 16, spread_step, 0)
    block_copy.wait()
    tile = ((iota((16, 1024), 1) & 15) == iota((16, 1024), 0)).astype(F32).astype(BF16)
    repeat = ((iota((256, 16), 0) >> 4) == iota((256, 16), 1)).astype(F32).astype(BF16)
    for g in range(2):
        for q in range(2):
            left = lax.dot_general(
                blocks[g * 16:(g + 1) * 16, q * 256:(q + 1) * 256], tile, TN, preferred_element_type=F32
            )
            p0 = g * 32 + q * 16
            right = dot(repeat, spread_rows[p0:p0 + 16, :].astype(BF16))
            chan[p0 * 16:p0 * 16 + 256, :] = (left * right).astype(BF16)

    pltpu.make_async_copy(rows_at(recv1, 0, 16), rows_at(recv1, 0, 16), own_sem.at[0]).wait()
    pltpu.make_async_copy(rows_at(recv1, 0, 255 * 16), rows_at(recv1, 0, 255 * 16), recv1_sem).wait()

    def col_step(t, carry):
        pair = pair_of((x + t // 4) % 4, (y + t % 4) % 4)
        weights = expand[pl.ds(pl.multiple_of(pair * 256, 256), 256), :]
        low = dot(weights, recv1[0:2048, :]).astype(BF16)
        high = dot(weights, recv1[2048:4096, :]).astype(BF16)
        for h in range(2):
            cut = slice(h * 512, (h + 1) * 512)
            mixed = dot(low, chan[0:512, cut]) + dot(high, chan[512:1024, cut])
            send2[pl.ds(pl.multiple_of((pair * 2 + h) * 256, 256), 256), :] = mixed.astype(BF16)
        send_tile(
            pair, send2, (recv2, mine), recv2_sem.at[t],
            lambda half, far_z, far_core: (pair * 2 + far_z // 4) * 16 + half * 8 + (far_z % 4) * 2 + far_core,
            own_sem.at[1],
        )
        return carry

    lax.fori_loop(0, 8, col_step, 0)
    pltpu.make_async_copy(rows_at(recv2, 0, 16), rows_at(recv2, 0, 16), own_sem.at[1]).wait()

    def last_step(t, own):
        pair = pair_of((x - t // 4 + 4) % 4, (y - t % 4 + 4) % 4)
        got = rows_at(recv2, pair * 512, 512 - own)
        pltpu.make_async_copy(got, got, recv2_sem.at[t]).wait()
        spread = dot(unweave[...], recv2[pl.ds(pl.multiple_of(pair * 512, 512), 512), :])
        for i in range(4):
            part = pl.ds(pl.multiple_of(i * 1024 + pair * 128, 128), 128)
            out[part, :] = (signal[part, :].astype(F32) + gates[part, :] * spread[i * 128:(i + 1) * 128, :]).astype(BF16)

    last_step(0, 16)

    def rest(t, carry):
        last_step(t, 0)
        return carry

    lax.fori_loop(1, 8, rest, 0)
    pltpu.make_async_copy(rows_at(send1, 0, 255 * 16), rows_at(send1, 0, 255 * 16), send_sem).wait()
    pltpu.make_async_copy(rows_at(send2, 0, 255 * 16), rows_at(send2, 0, 255 * 16), send_sem).wait()


def per_device(signal, twiddle, row_factor, col_factor, block_mix, spread_mix, gate_scale):
    groups, width, _ = block_mix.shape
    anywhere = pl.BlockSpec(memory_space=pl.ANY)
    inside = pl.BlockSpec(memory_space=pltpu.VMEM)
    dma = pltpu.SemaphoreType.DMA
    return pl.pallas_call(
        kernel,
        out_shape=pltpu.VMEM(signal.shape, signal.dtype),
        in_specs=[anywhere, anywhere, anywhere, inside, inside, inside, inside],
        out_specs=inside,
        scratch_shapes=[
            pltpu.VMEM((4096, 512), BF16),
            pltpu.VMEM((1024, 1024), BF16),
            pltpu.VMEM((512, 512), BF16),
            pltpu.VMEM((4096, 512), BF16),
            pltpu.VMEM((4096, 512), BF16),
            pltpu.VMEM((2048, 2048), BF16),
            pltpu.VMEM((1024, 1024), BF16),
            pltpu.VMEM((4096, 512), BF16),
            pltpu.VMEM((4096, 512), BF16),
            pltpu.VMEM((4096, 512), F32),
            pltpu.VMEM((512, 512), BF16),
            pltpu.VMEM((512, 512), BF16),
            pltpu.VMEM((32, 512), BF16),
            pltpu.VMEM((64, 1024), F32),
            dma((6,)), dma((2,)), dma, dma, dma((8,)), dma((2,)), pltpu.SemaphoreType.REGULAR,
        ],
        compiler_params=pltpu.CompilerParams(
            collective_id=0, has_side_effects=True, vmem_limit_bytes=52 << 20),
    )(
        signal, row_factor, col_factor, twiddle, block_mix.transpose(1, 2, 0).reshape(width * width, groups),
        spread_mix.reshape(-1, spread_mix.shape[2]), gate_scale.reshape(1, -1),
    )


def solution(mesh):
    placed = (P("seq", "ch"), P("seq", None), P(), P(), P("ch", None, None), P(), P("ch"))
    return jax.shard_map(
        per_device, mesh=mesh, in_specs=placed, out_specs=P("seq", "ch"), check_vma=False
    )
```

```python
import jax
import jax.numpy as jnp
from jax import lax
from jax.experimental import pallas as pl
from jax.experimental.pallas import tpu as pltpu
from jax.sharding import PartitionSpec as P

F32 = jnp.float32
BF16 = jnp.bfloat16
NT = (((1,), (1,)), ((), ()))
TN = (((0,), (0,)), ((), ()))


def iota(shape, dim):
    return lax.broadcasted_iota(jnp.int32, shape, dim)


def dot(a, b):
    return jnp.dot(a, b, preferred_element_type=F32)


def rows_at(ref, start, size):
    return ref.at[pl.ds(pl.multiple_of(start, 16), size)]


def group_of(core, x, y):
    return core * 4 + (x % 2) * 2 + y % 2


def z_offset(n):
    odd = n % 2
    step = odd * ((n + 1) // 2) + (1 - odd) * (8 - n // 2)
    return (step - 4 * jnp.where(n == 0, 1, 0) + jnp.where(n == 7, 4, 0)) % 8


def kernel(
    signal_hbm, rowf_hbm, colf_hbm, tw_ref, block_ref, mix_ref, gate_ref,
    out,
    signal, rowf, colf, send1, recv1, expand, chan, send2, recv2, gates,
    weave, unweave, blocks, spread_rows,
    load_sem, send_sem, recv1_sem, recv2_sem, block_sem, plane_sem,
):
    seq, ch = lax.axis_index("seq"), lax.axis_index("ch")
    y, x, core = seq // 32, (seq // 2) % 4, seq % 2
    z = ch * 4 + (seq // 8) % 4
    mine = group_of(core, x, y) * 32 + (x // 2) * 16 + (y // 2) * 8 + z

    barrier = pltpu.get_barrier_semaphore()

    def greet(sem, dx, dy, dz, dc):
        far_z = (z + dz) % 8
        far_seq = (y + dy) % 4 * 32 + far_z % 4 * 8 + (x + dx) % 4 * 2 + (core + dc) % 2
        pl.semaphore_signal(
            sem, inc=1, device_id=(far_seq, far_z // 4), device_id_type=pl.DeviceIdType.MESH
        )

    def greet_plane(sem):
        def body(n, carry):
            greet(sem, (n + 1) % 4, (n + 1) // 4, 0, 0)
            return carry

        lax.fori_loop(0, 15, body, 0)

    def greet_line(n, carry):
        greet(barrier, 0, 0, (n + 1) // 2, (n + 1) % 2)
        return carry

    loads = []
    for i in range(4):
        part = pl.ds(i * 1024, 1024)
        loads.append(pltpu.make_async_copy(signal_hbm.at[part], signal.at[part], load_sem.at[1 + i]))
    loads = [pltpu.make_async_copy(rowf_hbm, rowf, load_sem.at[0])] + loads
    loads.append(pltpu.make_async_copy(colf_hbm, colf, load_sem.at[5]))
    lax.fori_loop(0, 15, greet_line, 0)
    greet_plane(barrier)
    for load in loads:
        load.start()

    o, s = iota((512, 512), 0), iota((512, 512), 1)
    weave[...] = (s == ((o >> 2) & 3) * 128 + (o >> 4) * 4 + (o & 3)).astype(F32).astype(BF16)
    eye = iota((128, 128), 0) == iota((128, 128), 1)
    eye16 = eye.astype(F32).astype(BF16)

    flipped = jnp.zeros((16, 512), F32)
    for q in range(16):
        place = (iota((32, 512), 1) == iota((32, 512), 0) * 16 + q).astype(F32).astype(BF16)
        flipped += dot(block_ref[q * 16:(q + 1) * 16, :], place)
    blocks[pl.ds(pl.multiple_of(ch * 16, 16), 16), :] = flipped.astype(BF16)
    block_copy = pltpu.make_async_remote_copy(
        src_ref=rows_at(blocks, ch * 16, 16), dst_ref=rows_at(blocks, ch * 16, 16),
        send_sem=block_sem.at[0], recv_sem=block_sem.at[1],
        device_id=(seq, 1 - ch), device_id_type=pl.DeviceIdType.MESH,
    )
    pl.semaphore_wait(barrier, 30)
    greet_plane(plane_sem)

    def send_tile(group, t, source, target, recv_sem, source_row):
        dst = rows_at(target[0], target[1] * 16, 16)

        def body(n, carry):
            far_x = (x + t // 2 % 2 + n // 16 * 2) % 4
            far_y = (y + t % 2 + n // 8 * 2) % 4
            far_z = (z + z_offset(n % 8)) % 8
            far_seq = far_y * 32 + (far_z % 4) * 8 + far_x * 2 + group // 4
            far_ch = far_z // 4
            src = rows_at(source, source_row(far_x // 2, far_y // 2, far_z) * 16, 16)
            is_self = jnp.logical_and(far_seq == seq, far_ch == ch)

            @pl.when(is_self)
            def _():
                pltpu.make_async_copy(src, dst, recv_sem).start()

            @pl.when(jnp.logical_not(is_self))
            def _():
                pltpu.make_async_remote_copy(
                    src_ref=src, dst_ref=dst, send_sem=send_sem, recv_sem=recv_sem,
                    device_id=(far_seq, far_ch), device_id_type=pl.DeviceIdType.MESH,
                ).start()

            return carry

        lax.fori_loop(0, 32, body, 0)

    def row_step(t, carry):
        group = group_of(t // 4, x + t // 2 % 2, y + t % 2)
        lanes = pl.ds(pl.multiple_of(group * 128, 128), 128)

        @pl.when(t == 0)
        def _():
            loads[0].wait()

        weights = lax.dot_general(eye16, rowf[:, lanes], NT, preferred_element_type=F32).astype(BF16)
        parts = []
        for i in range(4):
            @pl.when(t == 0)
            def _():
                loads[1 + i].wait()

            mixed = dot(weights, signal[i * 1024:(i + 1) * 1024, :])
            scale = jnp.sum(jnp.where(eye, tw_ref[i:i + 1, lanes], 0.0), axis=1, keepdims=True)
            parts.append((mixed * scale).astype(BF16))
        woven = dot(weave[...], jnp.concatenate(parts, axis=0)).astype(BF16)
        send1[pl.ds(pl.multiple_of(group * 512, 512), 512), :] = woven

        @pl.when(t == 0)
        def _():
            pl.semaphore_wait(plane_sem, 15)
            block_copy.start()

        send_tile(
            group, t, send1, (recv1, ch * 128 + seq), recv1_sem,
            lambda half_x, half_y, far_z: group * 32 + half_x * 16 + half_y * 8 + far_z,
        )
        return carry

    lax.fori_loop(0, 8, row_step, 0)

    loads[5].wait()

    def gate_step(n, carry):
        part = pl.ds(pl.multiple_of(n * 64, 64), 64)
        v = gate_ref[...] * signal[part, :].astype(F32)
        gates[part, :] = v / (1.0 + jnp.exp(-v))
        return carry

    lax.fori_loop(0, 64, gate_step, 0)

    def expand_step(group, carry):
        r = iota((256, 512), 0)
        far_x = group // 2 % 2 + 2 * (r >> 7)
        far_y = group % 2 + 2 * ((r >> 6) & 1)
        far_seq = far_y * 32 + ((r >> 4) & 3) * 8 + far_x * 2 + group // 4
        pick = (iota((256, 512), 1) == far_seq * 4 + ((r >> 2) & 3)).astype(F32).astype(BF16)
        taken = lax.dot_general(pick, colf[...], NT, preferred_element_type=F32).astype(BF16)
        widen = (iota((128, 512), 0) == (iota((128, 512), 1) >> 2)).astype(F32).astype(BF16)
        same = (iota((256, 512), 0) & 3) == (iota((256, 512), 1) & 3)
        rows = pl.ds(pl.multiple_of(group * 256, 256), 256)
        for j in range(4):
            wide = dot(taken[:, j * 128:(j + 1) * 128], widen)
            expand[rows, j * 512:(j + 1) * 512] = jnp.where(same, wide, 0.0).astype(BF16)
        return carry

    lax.fori_loop(0, 8, expand_step, 0)

    unweave[...] = (o == ((s >> 2) & 3) * 128 + (s >> 4) * 4 + (s & 3)).astype(F32).astype(BF16)
    spread_rows[...] = jnp.zeros_like(spread_rows)

    def spread_step(r, carry):
        place = (iota((64, 1024), 1) == iota((64, 1024), 0) * 16 + r).astype(F32).astype(BF16)
        spread_rows[...] += dot(mix_ref[pl.ds(pl.multiple_of(r * 64, 64), 64), :], place)
        return carry

    lax.fori_loop(0, 16, spread_step, 0)
    block_copy.wait()
    tile = ((iota((16, 1024), 1) & 15) == iota((16, 1024), 0)).astype(F32).astype(BF16)
    repeat = ((iota((256, 16), 0) >> 4) == iota((256, 16), 1)).astype(F32).astype(BF16)
    for g in range(2):
        for q in range(2):
            left = lax.dot_general(
                blocks[g * 16:(g + 1) * 16, q * 256:(q + 1) * 256], tile, TN, preferred_element_type=F32
            )
            p0 = g * 32 + q * 16
            right = dot(repeat, spread_rows[p0:p0 + 16, :].astype(BF16))
            chan[p0 * 16:p0 * 16 + 256, :] = (left * right).astype(BF16)

    pltpu.make_async_copy(recv1, recv1, recv1_sem).wait()

    def col_step(t, carry):
        group = group_of((core + t // 4) % 2, x + t // 2 % 2, y + t % 2)
        weights = expand[pl.ds(pl.multiple_of(group * 256, 256), 256), :]
        low = dot(weights, recv1[0:2048, :]).astype(BF16)
        high = dot(weights, recv1[2048:4096, :]).astype(BF16)
        for h in range(2):
            cut = slice(h * 512, (h + 1) * 512)
            mixed = dot(low, chan[0:512, cut]) + dot(high, chan[512:1024, cut])
            send2[pl.ds(pl.multiple_of((group * 2 + h) * 256, 256), 256), :] = mixed.astype(BF16)
        send_tile(
            group, t, send2, (recv2, mine), recv2_sem.at[t],
            lambda half_x, half_y, far_z: (group * 2 + far_z // 4) * 16 + half_x * 8 + half_y * 4 + far_z % 4,
        )
        return carry

    lax.fori_loop(0, 8, col_step, 0)

    def last_step(n, carry):
        t = (n + core * 4) % 8
        group = group_of(n // 4, x + t // 2 % 2, y + t % 2)
        got = rows_at(recv2, group * 512, 512)
        pltpu.make_async_copy(got, got, recv2_sem.at[t]).wait()
        spread = dot(unweave[...], recv2[pl.ds(pl.multiple_of(group * 512, 512), 512), :])
        for i in range(4):
            part = pl.ds(pl.multiple_of(i * 1024 + group * 128, 128), 128)
            out[part, :] = (signal[part, :].astype(F32) + gates[part, :] * spread[i * 128:(i + 1) * 128, :]).astype(BF16)

        return carry

    lax.fori_loop(0, 8, last_step, 0)
    pltpu.make_async_copy(rows_at(send1, 0, 255 * 16), rows_at(send1, 0, 255 * 16), send_sem).wait()
    pltpu.make_async_copy(rows_at(send2, 0, 255 * 16), rows_at(send2, 0, 255 * 16), send_sem).wait()


def per_device(signal, twiddle, row_factor, col_factor, block_mix, spread_mix, gate_scale):
    groups, width, _ = block_mix.shape
    anywhere = pl.BlockSpec(memory_space=pl.ANY)
    inside = pl.BlockSpec(memory_space=pltpu.VMEM)
    dma = pltpu.SemaphoreType.DMA
    return pl.pallas_call(
        kernel,
        out_shape=pltpu.VMEM(signal.shape, signal.dtype),
        in_specs=[anywhere, anywhere, anywhere, inside, inside, inside, inside],
        out_specs=inside,
        scratch_shapes=[
            pltpu.VMEM((4096, 512), BF16),
            pltpu.VMEM((1024, 1024), BF16),
            pltpu.VMEM((512, 512), BF16),
            pltpu.VMEM((4096, 512), BF16),
            pltpu.VMEM((4096, 512), BF16),
            pltpu.VMEM((2048, 2048), BF16),
            pltpu.VMEM((1024, 1024), BF16),
            pltpu.VMEM((4096, 512), BF16),
            pltpu.VMEM((4096, 512), BF16),
            pltpu.VMEM((4096, 512), F32),
            pltpu.VMEM((512, 512), BF16),
            pltpu.VMEM((512, 512), BF16),
            pltpu.VMEM((32, 512), BF16),
            pltpu.VMEM((64, 1024), F32),
            dma((6,)), dma, dma, dma((8,)), dma((2,)), pltpu.SemaphoreType.REGULAR,
        ],
        compiler_params=pltpu.CompilerParams(
            collective_id=0, has_side_effects=True, vmem_limit_bytes=52 << 20),
    )(
        signal, row_factor, col_factor, twiddle, block_mix.transpose(1, 2, 0).reshape(width * width, groups),
        spread_mix.reshape(-1, spread_mix.shape[2]), gate_scale.reshape(1, -1),
    )


def solution(mesh):
    placed = (P("seq", "ch"), P("seq", None), P(), P(), P("ch", None, None), P(), P("ch"))
    return jax.shard_map(
        per_device, mesh=mesh, in_specs=placed, out_specs=P("seq", "ch"), check_vma=False
    )
```

```python
import jax
import jax.numpy as jnp
from jax import lax
from jax.experimental import pallas as pl
from jax.experimental.pallas import tpu as pltpu
from jax.sharding import PartitionSpec as P

F32 = jnp.float32
BF16 = jnp.bfloat16
NT = (((1,), (1,)), ((), ()))
TN = (((0,), (0,)), ((), ()))


def iota(shape, dim):
    return lax.broadcasted_iota(jnp.int32, shape, dim)


def dot(a, b):
    return jnp.dot(a, b, preferred_element_type=F32)


def rows_at(ref, start, size):
    return ref.at[pl.ds(pl.multiple_of(start, 16), size)]


def group_of(core, x, y):
    return core * 4 + (x % 2) * 2 + y % 2


def z_offset(n):
    odd = n % 2
    step = odd * ((n + 1) // 2) + (1 - odd) * (8 - n // 2)
    return (step - 4 * jnp.where(n == 0, 1, 0) + jnp.where(n == 7, 4, 0)) % 8


def kernel(
    signal_hbm, rowf_hbm, colf_hbm, tw_hbm, block_hbm, mix_hbm, gate_hbm,
    out,
    signal, rowf, colf, send1, recv1, expand, chan, send2, recv2, gates,
    weave, unweave, blocks, spread_rows, tw_ref, block_ref, mix_ref, gate_ref, rowf_first, weights,
    load_sem, send_sem, recv1_sem, recv2_sem, block_sem, plane_sem,
):
    seq, ch = lax.axis_index("seq"), lax.axis_index("ch")
    y, x, core = seq // 32, (seq // 2) % 4, seq % 2
    z = ch * 4 + (seq // 8) % 4
    mine = group_of(core, x, y) * 32 + (x // 2) * 16 + (y // 2) * 8 + z

    barrier = pltpu.get_barrier_semaphore()

    def greet(sem, dx, dy, dz, dc):
        far_z = (z + dz) % 8
        far_seq = (y + dy) % 4 * 32 + far_z % 4 * 8 + (x + dx) % 4 * 2 + (core + dc) % 2
        pl.semaphore_signal(
            sem, inc=1, device_id=(far_seq, far_z // 4), device_id_type=pl.DeviceIdType.MESH
        )

    def greet_plane(sem):
        def body(n, carry):
            greet(sem, (n + 1) % 4, (n + 1) // 4, 0, 0)
            return carry

        lax.fori_loop(0, 15, body, 0)

    def greet_line(n, carry):
        greet(barrier, 0, 0, (n + 1) // 2, (n + 1) % 2)
        return carry

    first = group_of(0, x, y)
    first_load = pltpu.make_async_copy(
        rowf_hbm.at[:, pl.ds(pl.multiple_of(first * 128, 128), 128)], rowf_first, load_sem.at[0]
    )
    loads = []
    for i in range(4):
        part = pl.ds(i * 1024, 1024)
        loads.append(pltpu.make_async_copy(signal_hbm.at[part], signal.at[part], load_sem.at[1 + i]))
    block_load = pltpu.make_async_copy(block_hbm, block_ref, load_sem.at[5])
    tw_load = pltpu.make_async_copy(tw_hbm, tw_ref, load_sem.at[6])
    rowf_load = pltpu.make_async_copy(rowf_hbm, rowf, load_sem.at[7])
    late_loads = [
        pltpu.make_async_copy(colf_hbm, colf, load_sem.at[8]),
        pltpu.make_async_copy(mix_hbm, mix_ref, load_sem.at[9]),
        pltpu.make_async_copy(gate_hbm, gate_ref, load_sem.at[10]),
    ]
    for load in [block_load, first_load, tw_load] + loads:
        load.start()
    lax.fori_loop(0, 15, greet_line, 0)
    greet_plane(barrier)
    for load in [rowf_load] + late_loads:
        load.start()

    def answer_line():
        pl.semaphore_wait(barrier, 30)
        greet_plane(plane_sem)

    far = z >= 4

    @pl.when(far)
    def _():
        answer_line()

    o, s = iota((512, 512), 0), iota((512, 512), 1)
    weave[...] = (s == ((o >> 2) & 3) * 128 + (o >> 4) * 4 + (o & 3)).astype(F32).astype(BF16)
    eye = iota((128, 128), 0) == iota((128, 128), 1)
    eye16 = eye.astype(F32).astype(BF16)

    block_load.wait()
    flipped = jnp.zeros((16, 512), F32)
    for q in range(16):
        place = (iota((32, 512), 1) == iota((32, 512), 0) * 16 + q).astype(F32).astype(BF16)
        flipped += dot(block_ref[q * 16:(q + 1) * 16, :], place)
    blocks[pl.ds(pl.multiple_of(ch * 16, 16), 16), :] = flipped.astype(BF16)
    block_copy = pltpu.make_async_remote_copy(
        src_ref=rows_at(blocks, ch * 16, 16), dst_ref=rows_at(blocks, ch * 16, 16),
        send_sem=block_sem.at[0], recv_sem=block_sem.at[1],
        device_id=(seq, 1 - ch), device_id_type=pl.DeviceIdType.MESH,
    )

    def send_tile(group, t, source, target, recv_sem, source_row, start=0, stop=32):
        dst = rows_at(target[0], target[1] * 16, 16)

        def body(n, carry):
            far_x = (x + t // 2 % 2 + n // 16 * 2) % 4
            far_y = (y + t % 2 + n // 8 * 2) % 4
            far_z = (z + z_offset(n % 8)) % 8
            far_seq = far_y * 32 + (far_z % 4) * 8 + far_x * 2 + group // 4
            far_ch = far_z // 4
            src = rows_at(source, source_row(far_x // 2, far_y // 2, far_z) * 16, 16)
            is_self = jnp.logical_and(far_seq == seq, far_ch == ch)

            @pl.when(is_self)
            def _():
                pltpu.make_async_copy(src, dst, recv_sem).start()

            @pl.when(jnp.logical_not(is_self))
            def _():
                pltpu.make_async_remote_copy(
                    src_ref=src, dst_ref=dst, send_sem=send_sem, recv_sem=recv_sem,
                    device_id=(far_seq, far_ch), device_id_type=pl.DeviceIdType.MESH,
                ).start()

            return carry

        lax.fori_loop(start, stop, body, 0)

    def row_step(t, carry):
        group = group_of(t // 4, x + t // 2 % 2, y + t % 2)
        lanes = pl.ds(pl.multiple_of(group * 128, 128), 128)

        @pl.when(t == 0)
        def _():
            first_load.wait()
            tw_load.wait()
            weights[...] = lax.dot_general(eye16, rowf_first[...], NT, preferred_element_type=F32).astype(BF16)

        @pl.when(t == 1)
        def _():
            rowf_load.wait()

        @pl.when(t > 0)
        def _():
            weights[...] = lax.dot_general(eye16, rowf[:, lanes], NT, preferred_element_type=F32).astype(BF16)

        parts = []
        for i in range(4):
            @pl.when(t == 0)
            def _():
                loads[i].wait()

            mixed = dot(weights[...], signal[i * 1024:(i + 1) * 1024, :])
            scale = jnp.sum(jnp.where(eye, tw_ref[i:i + 1, lanes], 0.0), axis=1, keepdims=True)
            parts.append((mixed * scale).astype(BF16))
        woven = dot(weave[...], jnp.concatenate(parts, axis=0)).astype(BF16)
        send1[pl.ds(pl.multiple_of(group * 512, 512), 512), :] = woven

        @pl.when(jnp.logical_and(t == 0, jnp.logical_not(far)))
        def _():
            answer_line()

        @pl.when(t == 0)
        def _():
            block_copy.start()

        def send_rows(start, stop):
            send_tile(
                group, t, send1, (recv1, ch * 128 + seq), recv1_sem,
                lambda half_x, half_y, far_z: group * 32 + half_x * 16 + half_y * 8 + far_z,
                start, stop,
            )

        send_rows(0, 8)

        @pl.when(t == 0)
        def _():
            pl.semaphore_wait(plane_sem, 15)

        send_rows(8, 32)
        return carry

    lax.fori_loop(0, 8, row_step, 0)

    for load in late_loads:
        load.wait()

    def gate_step(n, carry):
        part = pl.ds(pl.multiple_of(n * 64, 64), 64)
        v = gate_ref[...] * signal[part, :].astype(F32)
        gates[part, :] = v / (1.0 + jnp.exp(-v))
        return carry

    lax.fori_loop(0, 64, gate_step, 0)

    def expand_step(group, carry):
        r = iota((256, 512), 0)
        far_x = group // 2 % 2 + 2 * (r >> 7)
        far_y = group % 2 + 2 * ((r >> 6) & 1)
        far_seq = far_y * 32 + ((r >> 4) & 3) * 8 + far_x * 2 + group // 4
        pick = (iota((256, 512), 1) == far_seq * 4 + ((r >> 2) & 3)).astype(F32).astype(BF16)
        taken = lax.dot_general(pick, colf[...], NT, preferred_element_type=F32).astype(BF16)
        widen = (iota((128, 512), 0) == (iota((128, 512), 1) >> 2)).astype(F32).astype(BF16)
        same = (iota((256, 512), 0) & 3) == (iota((256, 512), 1) & 3)
        rows = pl.ds(pl.multiple_of(group * 256, 256), 256)
        for j in range(4):
            wide = dot(taken[:, j * 128:(j + 1) * 128], widen)
            expand[rows, j * 512:(j + 1) * 512] = jnp.where(same, wide, 0.0).astype(BF16)
        return carry

    lax.fori_loop(0, 8, expand_step, 0)

    unweave[...] = (o == ((s >> 2) & 3) * 128 + (s >> 4) * 4 + (s & 3)).astype(F32).astype(BF16)
    spread_rows[...] = jnp.zeros_like(spread_rows)

    def spread_step(r, carry):
        place = (iota((64, 1024), 1) == iota((64, 1024), 0) * 16 + r).astype(F32).astype(BF16)
        spread_rows[...] += dot(mix_ref[pl.ds(pl.multiple_of(r * 64, 64), 64), :], place)
        return carry

    lax.fori_loop(0, 16, spread_step, 0)
    block_copy.wait()
    tile = ((iota((16, 1024), 1) & 15) == iota((16, 1024), 0)).astype(F32).astype(BF16)
    repeat = ((iota((256, 16), 0) >> 4) == iota((256, 16), 1)).astype(F32).astype(BF16)
    for g in range(2):
        for q in range(2):
            left = lax.dot_general(
                blocks[g * 16:(g + 1) * 16, q * 256:(q + 1) * 256], tile, TN, preferred_element_type=F32
            )
            p0 = g * 32 + q * 16
            right = dot(repeat, spread_rows[p0:p0 + 16, :].astype(BF16))
            chan[p0 * 16:p0 * 16 + 256, :] = (left * right).astype(BF16)

    pltpu.make_async_copy(recv1, recv1, recv1_sem).wait()

    def col_step(t, carry):
        group = group_of((core + t // 4) % 2, x + t // 2 % 2, y + t % 2)
        weights = expand[pl.ds(pl.multiple_of(group * 256, 256), 256), :]
        low = dot(weights, recv1[0:2048, :]).astype(BF16)
        high = dot(weights, recv1[2048:4096, :]).astype(BF16)
        for h in range(2):
            cut = slice(h * 512, (h + 1) * 512)
            mixed = dot(low, chan[0:512, cut]) + dot(high, chan[512:1024, cut])
            send2[pl.ds(pl.multiple_of((group * 2 + h) * 256, 256), 256), :] = mixed.astype(BF16)
        send_tile(
            group, t, send2, (recv2, mine), recv2_sem.at[t],
            lambda half_x, half_y, far_z: (group * 2 + far_z // 4) * 16 + half_x * 8 + half_y * 4 + far_z % 4,
        )
        return carry

    lax.fori_loop(0, 8, col_step, 0)

    def last_step(n, carry):
        t = (n + core * 4) % 8
        group = group_of(n // 4, x + t // 2 % 2, y + t % 2)
        got = rows_at(recv2, group * 512, 512)
        pltpu.make_async_copy(got, got, recv2_sem.at[t]).wait()
        spread = dot(unweave[...], recv2[pl.ds(pl.multiple_of(group * 512, 512), 512), :])
        for i in range(4):
            part = pl.ds(pl.multiple_of(i * 1024 + group * 128, 128), 128)
            out[part, :] = (signal[part, :].astype(F32) + gates[part, :] * spread[i * 128:(i + 1) * 128, :]).astype(BF16)

        return carry

    lax.fori_loop(0, 8, last_step, 0)
    pltpu.make_async_copy(rows_at(send1, 0, 255 * 16), rows_at(send1, 0, 255 * 16), send_sem).wait()
    pltpu.make_async_copy(rows_at(send2, 0, 255 * 16), rows_at(send2, 0, 255 * 16), send_sem).wait()


def per_device(signal, twiddle, row_factor, col_factor, block_mix, spread_mix, gate_scale):
    groups, width, _ = block_mix.shape
    anywhere = pl.BlockSpec(memory_space=pl.ANY)
    inside = pl.BlockSpec(memory_space=pltpu.VMEM)
    dma = pltpu.SemaphoreType.DMA
    return pl.pallas_call(
        kernel,
        out_shape=pltpu.VMEM(signal.shape, signal.dtype),
        in_specs=[anywhere] * 7,
        out_specs=inside,
        scratch_shapes=[
            pltpu.VMEM((4096, 512), BF16),
            pltpu.VMEM((1024, 1024), BF16),
            pltpu.VMEM((512, 512), BF16),
            pltpu.VMEM((4096, 512), BF16),
            pltpu.VMEM((4096, 512), BF16),
            pltpu.VMEM((2048, 2048), BF16),
            pltpu.VMEM((1024, 1024), BF16),
            pltpu.VMEM((4096, 512), BF16),
            pltpu.VMEM((4096, 512), BF16),
            pltpu.VMEM((4096, 512), F32),
            pltpu.VMEM((512, 512), BF16),
            pltpu.VMEM((512, 512), BF16),
            pltpu.VMEM((32, 512), BF16),
            pltpu.VMEM((64, 1024), F32),
            pltpu.VMEM((4, 1024), F32),
            pltpu.VMEM((256, 32), BF16),
            pltpu.VMEM((1024, 64), BF16),
            pltpu.VMEM((1, 512), F32),
            pltpu.VMEM((1024, 128), BF16),
            pltpu.VMEM((128, 1024), BF16),
            dma((11,)), dma, dma, dma((8,)), dma((2,)), pltpu.SemaphoreType.REGULAR,
        ],
        compiler_params=pltpu.CompilerParams(
            collective_id=0, has_side_effects=True, vmem_limit_bytes=52 << 20),
    )(
        signal, row_factor, col_factor, twiddle, block_mix.transpose(1, 2, 0).reshape(width * width, groups),
        spread_mix.reshape(-1, spread_mix.shape[2]), gate_scale.reshape(1, -1),
    )


def solution(mesh):
    placed = (P("seq", "ch"), P("seq", None), P(), P(), P("ch", None, None), P(), P("ch"))
    return jax.shard_map(
        per_device, mesh=mesh, in_specs=placed, out_specs=P("seq", "ch"), check_vma=False
    )
```

```python
import jax
import jax.numpy as jnp
from jax import lax
from jax.experimental import pallas as pl
from jax.experimental.pallas import tpu as pltpu
from jax.sharding import PartitionSpec as P

F32 = jnp.float32
BF16 = jnp.bfloat16
NT = (((1,), (1,)), ((), ()))
TN = (((0,), (0,)), ((), ()))


def iota(shape, dim):
    return lax.broadcasted_iota(jnp.int32, shape, dim)


def dot(a, b):
    return jnp.dot(a, b, preferred_element_type=F32)


def rows_at(ref, start, size):
    return ref.at[pl.ds(pl.multiple_of(start, 16), size)]


def group_of(core, x, y):
    return core * 4 + (x % 2) * 2 + y % 2


def z_offset(n):
    odd = n % 2
    step = odd * ((n + 1) // 2) + (1 - odd) * (8 - n // 2)
    return (step - 4 * jnp.where(n == 0, 1, 0) + jnp.where(n == 7, 4, 0)) % 8


def kernel(
    signal_hbm, rowf_hbm, colf_hbm, tw_hbm, block_hbm, mix_hbm, gate_hbm,
    out,
    signal, rowf, colf, send1, recv1, expand, chan, send2, recv2, gates,
    weave, unweave, blocks, spread_rows, tw_ref, block_ref, mix_ref, gate_ref, rowf_first, weights,
    load_sem, send_sem, recv1_sem, recv2_sem, block_sem, plane_sem,
):
    seq, ch = lax.axis_index("seq"), lax.axis_index("ch")
    y, x, core = seq // 32, (seq // 2) % 4, seq % 2
    z = ch * 4 + (seq // 8) % 4
    mine = group_of(core, x, y) * 32 + (x // 2) * 16 + (y // 2) * 8 + z

    barrier = pltpu.get_barrier_semaphore()

    def greet(sem, dx, dy, dz, dc):
        far_z = (z + dz) % 8
        far_seq = (y + dy) % 4 * 32 + far_z % 4 * 8 + (x + dx) % 4 * 2 + (core + dc) % 2
        pl.semaphore_signal(
            sem, inc=1, device_id=(far_seq, far_z // 4), device_id_type=pl.DeviceIdType.MESH
        )

    def greet_plane(sem):
        def body(n, carry):
            greet(sem, (n + 1) % 4, (n + 1) // 4, 0, 0)
            return carry

        lax.fori_loop(0, 15, body, 0)

    def greet_line(n, carry):
        greet(barrier, 0, 0, (n + 1) // 2, (n + 1) % 2)
        return carry

    first = group_of(0, x, y)
    first_load = pltpu.make_async_copy(
        rowf_hbm.at[:, pl.ds(pl.multiple_of(first * 128, 128), 128)], rowf_first, load_sem.at[0]
    )
    loads = []
    for i in range(4):
        part = pl.ds(i * 1024, 1024)
        loads.append(pltpu.make_async_copy(signal_hbm.at[part], signal.at[part], load_sem.at[1 + i]))
    block_load = pltpu.make_async_copy(block_hbm, block_ref, load_sem.at[5])
    tw_load = pltpu.make_async_copy(tw_hbm, tw_ref, load_sem.at[6])
    rowf_load = pltpu.make_async_copy(rowf_hbm, rowf, load_sem.at[7])
    late_loads = [
        pltpu.make_async_copy(colf_hbm, colf, load_sem.at[8]),
        pltpu.make_async_copy(mix_hbm, mix_ref, load_sem.at[9]),
        pltpu.make_async_copy(gate_hbm, gate_ref, load_sem.at[10]),
    ]
    for load in [block_load, first_load, tw_load] + loads:
        load.start()
    lax.fori_loop(0, 15, greet_line, 0)
    greet_plane(barrier)
    for load in [rowf_load] + late_loads:
        load.start()

    def answer_line():
        pl.semaphore_wait(barrier, 30)
        greet_plane(plane_sem)

    far = z >= 4

    @pl.when(far)
    def _():
        answer_line()

    o, s = iota((512, 512), 0), iota((512, 512), 1)
    weave[...] = (s == ((o >> 2) & 3) * 128 + (o >> 4) * 4 + (o & 3)).astype(F32).astype(BF16)
    eye = iota((128, 128), 0) == iota((128, 128), 1)
    eye16 = eye.astype(F32).astype(BF16)

    block_load.wait()
    flipped = jnp.zeros((16, 512), F32)
    for q in range(16):
        place = (iota((32, 512), 1) == iota((32, 512), 0) * 16 + q).astype(F32).astype(BF16)
        flipped += dot(block_ref[q * 16:(q + 1) * 16, :], place)
    blocks[pl.ds(pl.multiple_of(ch * 16, 16), 16), :] = flipped.astype(BF16)
    block_copy = pltpu.make_async_remote_copy(
        src_ref=rows_at(blocks, ch * 16, 16), dst_ref=rows_at(blocks, ch * 16, 16),
        send_sem=block_sem.at[0], recv_sem=block_sem.at[1],
        device_id=(seq, 1 - ch), device_id_type=pl.DeviceIdType.MESH,
    )

    def send_one(group, dx, dy, half_x, half_y, far_z, source, source_row, target, recv_sem):
        far_x, far_y = (x + dx + half_x * 2) % 4, (y + dy + half_y * 2) % 4
        far_seq = far_y * 32 + (far_z % 4) * 8 + far_x * 2 + group // 4
        far_ch = far_z // 4
        src = rows_at(source, source_row(far_x // 2, far_y // 2) * 16, 16)
        dst = rows_at(target[0], target[1] * 16, 16)
        is_self = jnp.logical_and(far_seq == seq, far_ch == ch)

        @pl.when(is_self)
        def _():
            pltpu.make_async_copy(src, dst, recv_sem).start()

        @pl.when(jnp.logical_not(is_self))
        def _():
            pltpu.make_async_remote_copy(
                src_ref=src, dst_ref=dst, send_sem=send_sem, recv_sem=recv_sem,
                device_id=(far_seq, far_ch), device_id_type=pl.DeviceIdType.MESH,
            ).start()

    def row_step(t, carry):
        group = group_of(t // 4, x + t // 2 % 2, y + t % 2)
        lanes = pl.ds(pl.multiple_of(group * 128, 128), 128)

        @pl.when(t == 0)
        def _():
            first_load.wait()
            tw_load.wait()
            weights[...] = lax.dot_general(eye16, rowf_first[...], NT, preferred_element_type=F32).astype(BF16)

        @pl.when(t == 1)
        def _():
            rowf_load.wait()

        @pl.when(t > 0)
        def _():
            weights[...] = lax.dot_general(eye16, rowf[:, lanes], NT, preferred_element_type=F32).astype(BF16)

        parts = []
        for i in range(4):
            @pl.when(t == 0)
            def _():
                loads[i].wait()

            mixed = dot(weights[...], signal[i * 1024:(i + 1) * 1024, :])
            scale = jnp.sum(jnp.where(eye, tw_ref[i:i + 1, lanes], 0.0), axis=1, keepdims=True)
            parts.append((mixed * scale).astype(BF16))
        woven = dot(weave[...], jnp.concatenate(parts, axis=0)).astype(BF16)
        send1[pl.ds(pl.multiple_of(group * 512, 512), 512), :] = woven

        @pl.when(jnp.logical_and(t == 0, jnp.logical_not(far)))
        def _():
            answer_line()

        @pl.when(t == 0)
        def _():
            block_copy.start()

        def send_row(n, carry):
            far_z = (z + z_offset(n % 8)) % 8
            send_one(
                group, t // 2 % 2, t % 2, n // 16, n // 8 % 2, far_z, send1,
                lambda half_x, half_y: group * 32 + half_x * 16 + half_y * 8 + far_z,
                (recv1, ch * 128 + seq), recv1_sem,
            )
            return carry

        lax.fori_loop(0, 8, send_row, 0)

        @pl.when(t == 0)
        def _():
            pl.semaphore_wait(plane_sem, 15)

        lax.fori_loop(8, 32, send_row, 0)
        return carry

    lax.fori_loop(0, 8, row_step, 0)

    for load in late_loads:
        load.wait()

    def gate_step(n, carry):
        part = pl.ds(pl.multiple_of(n * 64, 64), 64)
        v = gate_ref[...] * signal[part, :].astype(F32)
        gates[part, :] = v / (1.0 + jnp.exp(-v))
        return carry

    lax.fori_loop(0, 64, gate_step, 0)

    def expand_step(group, carry):
        r = iota((256, 512), 0)
        far_x = group // 2 % 2 + 2 * (r >> 7)
        far_y = group % 2 + 2 * ((r >> 6) & 1)
        far_seq = far_y * 32 + ((r >> 4) & 3) * 8 + far_x * 2 + group // 4
        pick = (iota((256, 512), 1) == far_seq * 4 + ((r >> 2) & 3)).astype(F32).astype(BF16)
        taken = lax.dot_general(pick, colf[...], NT, preferred_element_type=F32).astype(BF16)
        widen = (iota((128, 512), 0) == (iota((128, 512), 1) >> 2)).astype(F32).astype(BF16)
        same = (iota((256, 512), 0) & 3) == (iota((256, 512), 1) & 3)
        rows = pl.ds(pl.multiple_of(group * 256, 256), 256)
        for j in range(4):
            wide = dot(taken[:, j * 128:(j + 1) * 128], widen)
            expand[rows, j * 512:(j + 1) * 512] = jnp.where(same, wide, 0.0).astype(BF16)
        return carry

    lax.fori_loop(0, 8, expand_step, 0)

    unweave[...] = (o == ((s >> 2) & 3) * 128 + (s >> 4) * 4 + (s & 3)).astype(F32).astype(BF16)
    spread_rows[...] = jnp.zeros_like(spread_rows)

    def spread_step(r, carry):
        place = (iota((64, 1024), 1) == iota((64, 1024), 0) * 16 + r).astype(F32).astype(BF16)
        spread_rows[...] += dot(mix_ref[pl.ds(pl.multiple_of(r * 64, 64), 64), :], place)
        return carry

    lax.fori_loop(0, 16, spread_step, 0)
    block_copy.wait()
    tile = ((iota((16, 1024), 1) & 15) == iota((16, 1024), 0)).astype(F32).astype(BF16)
    repeat = ((iota((256, 16), 0) >> 4) == iota((256, 16), 1)).astype(F32).astype(BF16)
    for g in range(2):
        for q in range(2):
            left = lax.dot_general(
                blocks[g * 16:(g + 1) * 16, q * 256:(q + 1) * 256], tile, TN, preferred_element_type=F32
            )
            p0 = g * 32 + q * 16
            right = dot(repeat, spread_rows[p0:p0 + 16, :].astype(BF16))
            chan[p0 * 16:p0 * 16 + 256, :] = (left * right).astype(BF16)

    pltpu.make_async_copy(recv1, recv1, recv1_sem).wait()

    def col_step(t, carry):
        group = group_of((core + t) % 2, x + t // 4, y + t // 2 % 2)
        weights = expand[pl.ds(pl.multiple_of(group * 256, 256), 256), :]
        low = dot(weights, recv1[0:2048, :]).astype(BF16)
        high = dot(weights, recv1[2048:4096, :]).astype(BF16)
        for h in range(2):
            cut = slice(h * 512, (h + 1) * 512)
            mixed = dot(low, chan[0:512, cut]) + dot(high, chan[512:1024, cut])
            send2[pl.ds(pl.multiple_of((group * 2 + h) * 256, 256), 256), :] = mixed.astype(BF16)

        @pl.when(t < 6)
        def _():
            def body(n, carry):
                send_col(t, n // 8, (z + z_offset(n % 8)) % 8)
                return carry

            lax.fori_loop(0, 32, body, 0)

        @pl.when(t == 7)
        def _():
            lax.fori_loop(0, 64, send_last, 0)

        return carry

    def send_col(t, quarter, far_z):
        group = group_of((core + t) % 2, x + t // 4, y + t // 2 % 2)
        send_one(
            group, t // 4, t // 2 % 2, quarter // 2, quarter % 2, far_z, send2,
            lambda half_x, half_y: (group * 2 + far_z // 4) * 16 + half_x * 8 + half_y * 4 + far_z % 4,
            (recv2, mine), recv2_sem.at[t],
        )

    def send_last(n, carry):
        m = n // 2
        send_col(6 + n % 2, m % 16 // 4, m // 16 * 4 + m % 4)
        return carry

    lax.fori_loop(0, 8, col_step, 0)

    def last_step(n, carry):
        t = n % 4 * 2 + (core + n // 4) % 2
        group = group_of(n // 4, x + t // 4, y + t // 2 % 2)
        got = rows_at(recv2, group * 512, 512)
        pltpu.make_async_copy(got, got, recv2_sem.at[t]).wait()
        spread = dot(unweave[...], recv2[pl.ds(pl.multiple_of(group * 512, 512), 512), :])
        for i in range(4):
            part = pl.ds(pl.multiple_of(i * 1024 + group * 128, 128), 128)
            out[part, :] = (signal[part, :].astype(F32) + gates[part, :] * spread[i * 128:(i + 1) * 128, :]).astype(BF16)

        return carry

    lax.fori_loop(0, 8, last_step, 0)
    pltpu.make_async_copy(rows_at(send1, 0, 255 * 16), rows_at(send1, 0, 255 * 16), send_sem).wait()
    pltpu.make_async_copy(rows_at(send2, 0, 255 * 16), rows_at(send2, 0, 255 * 16), send_sem).wait()


def per_device(signal, twiddle, row_factor, col_factor, block_mix, spread_mix, gate_scale):
    groups, width, _ = block_mix.shape
    anywhere = pl.BlockSpec(memory_space=pl.ANY)
    inside = pl.BlockSpec(memory_space=pltpu.VMEM)
    dma = pltpu.SemaphoreType.DMA
    return pl.pallas_call(
        kernel,
        out_shape=pltpu.VMEM(signal.shape, signal.dtype),
        in_specs=[anywhere] * 7,
        out_specs=inside,
        scratch_shapes=[
            pltpu.VMEM((4096, 512), BF16),
            pltpu.VMEM((1024, 1024), BF16),
            pltpu.VMEM((512, 512), BF16),
            pltpu.VMEM((4096, 512), BF16),
            pltpu.VMEM((4096, 512), BF16),
            pltpu.VMEM((2048, 2048), BF16),
            pltpu.VMEM((1024, 1024), BF16),
            pltpu.VMEM((4096, 512), BF16),
            pltpu.VMEM((4096, 512), BF16),
            pltpu.VMEM((4096, 512), F32),
            pltpu.VMEM((512, 512), BF16),
            pltpu.VMEM((512, 512), BF16),
            pltpu.VMEM((32, 512), BF16),
            pltpu.VMEM((64, 1024), F32),
            pltpu.VMEM((4, 1024), F32),
            pltpu.VMEM((256, 32), BF16),
            pltpu.VMEM((1024, 64), BF16),
            pltpu.VMEM((1, 512), F32),
            pltpu.VMEM((1024, 128), BF16),
            pltpu.VMEM((128, 1024), BF16),
            dma((11,)), dma, dma, dma((8,)), dma((2,)), pltpu.SemaphoreType.REGULAR,
        ],
        compiler_params=pltpu.CompilerParams(
            collective_id=0, has_side_effects=True, vmem_limit_bytes=52 << 20),
    )(
        signal, row_factor, col_factor, twiddle, block_mix.transpose(1, 2, 0).reshape(width * width, groups),
        spread_mix.reshape(-1, spread_mix.shape[2]), gate_scale.reshape(1, -1),
    )


def solution(mesh):
    placed = (P("seq", "ch"), P("seq", None), P(), P(), P("ch", None, None), P(), P("ch"))
    return jax.shard_map(
        per_device, mesh=mesh, in_specs=placed, out_specs=P("seq", "ch"), check_vma=False
    )
```
